32 devices in a mesh: dp: 8 (over z, core), tensor: 4 (over y, x).
Axes of the slice: x: 2, y: 2, z: 4, core: 2. Of those that a mesh axis runs over, the one named last changes fastest.
Arguments:
- activations: bfloat16 [8192, 8192], P('dp'), may hold values from -6 to 6
- out_grad: bfloat16 [8192, 28672], P('dp', 'tensor'), may hold values from -0.06591797 to 0.06591797
- projector: bfloat16 [8192, 512], P(('dp', 'tensor')), may hold values from -0.0625 to 0.0625
- first_moment: float32 [512, 28672], P('dp', 'tensor'), may hold values from -3 to 3
- second_moment: float32 [512, 28672], P('dp', 'tensor'), may hold values from 0.1 to 4
Outputs:
- update: float32 [8192, 28672], P('dp', 'tensor')
- new_first: float32 [512, 28672], P('dp', 'tensor')
- new_second: float32 [512, 28672], P('dp', 'tensor')
The draws below stay inside these ranges and needn't reach their ends.
All inputs are finite; a program needn't handle non-finite values.
Results may differ from the reference program's by a relative error of at most 0.0031.
Values may be sent and summed in bfloat16 or wider, within the bound.
No kernel may reach another device: no remote copies, remote signals or barrier semaphores. Data moves between devices by JAX's collectives and lax.ppermute only.
A program may use at most 192 MiB of HBM per device.

```python
import math
import jax
import jax.numpy as jnp
from jax import lax

D = 8192
FF = 28672
RANK = 512
TOKENS = 8192


def levels(stream_key, shape, pieces, smallest, top_value):
    gain, own = 1.0, jax.random.fold_in(stream_key, 6)
    for dim, shards_of in pieces:
        steps = jnp.exp(jax.random.uniform(jax.random.fold_in(own, dim), (shards_of,), jnp.float32, smallest / len(pieces), top_value / len(pieces)))
        gain = gain * jnp.repeat(steps, shape[dim] // shards_of).reshape([-1 if axis == dim else 1 for axis in range(len(shape))])
    return gain


def noise(rng, dims, spread, bound, pieces=(), held_as=jnp.bfloat16):
    result = jax.random.normal(rng, dims, jnp.float32) * spread
    if len(pieces) > 0:
        result = levels(rng, dims, pieces, -0.22, 0.18) * result
    return jnp.clip(result, min=-bound, max=bound).astype(held_as)


def setup_inputs(seed: int = 0) -> dict:
    key_of = jax.random.split(jax.random.key(seed), 6)
    return {
        "activations": noise(key_of[0], (TOKENS, D), 1.0, 6.0, ((0, 8),)),
        "out_grad": noise(key_of[1], (TOKENS, FF), (1.0 / TOKENS ** 0.5), 0.06591797, ((0, 8), (1, 4))),
        "projector": noise(key_of[2], (D, RANK), D ** -0.5, 0.0625, ((0, 32),)),
        "first_moment": noise(key_of[3], (RANK, FF), 0.5, 3.0, ((0, 8), (1, 4)), jnp.float32),
        "second_moment": jnp.clip(jnp.exp(math.log(4.0) - 3.6888794 * jax.random.uniform(key_of[4], (RANK, FF), jnp.float32) ** levels(key_of[4], (RANK, FF), ((0, 8), (1, 4)), -0.2, 0.2)), 0.1, 4.0),
    }


beta_one = 0.9
beta_two = 0.999
bias_one = 1.0 - 0.9 ** 10
bias_two = 1.0 - 0.999 ** 10
adam_eps = 1e-08

def reference(activations, out_grad, projector, first_moment, second_moment):
    projected = jnp.dot(activations, projector, preferred_element_type=jnp.float32).astype(jnp.bfloat16)
    coefficients = lax.dot_general(projected, out_grad, (((0,), (0,)), ((), ())), preferred_element_type=jnp.float32)
    new_first = beta_one * first_moment + (1.0 - beta_one) * coefficients
    new_second = beta_two * second_moment + (1.0 - beta_two) * coefficients * coefficients
    normalized = (new_first / bias_one / (jnp.sqrt(new_second / bias_two) + adam_eps)).astype(jnp.bfloat16)
    update = jnp.dot(projector, normalized, preferred_element_type=jnp.float32)
    return (update, new_first, new_second)
```

```python
import functools

import jax
import jax.numpy as jnp
from jax import lax
from jax.experimental import pallas as pl
from jax.experimental.pallas import tpu as pltpu
from jax.sharding import PartitionSpec as P

beta_one = 0.9
beta_two = 0.999
bias_one = 1.0 - 0.9**10
bias_two = 1.0 - 0.999**10
adam_eps = 1e-08

PARTS = 2
UNIT = 256
F32 = jnp.float32
BF16 = jnp.bfloat16
ANYWHERE = pl.BlockSpec(memory_space=pl.ANY)


def split_widths(columns):
    units, parts = columns // UNIT, min(PARTS, columns // UNIT)
    return [UNIT * (units // parts + (i < units % parts)) for i in range(parts)]


def params(mib):
    return pltpu.CompilerParams(vmem_limit_bytes=mib << 20)


def cost(flops, moved):
    return pl.CostEstimate(flops=flops, bytes_accessed=moved, transcendentals=0)


def gather(where, activations, many, depth):
    tokens = activations.shape[0]
    parts = max(1, 128 // depth)

    def body(where_ref, taken_ref, out_ref):
        for p in range(parts):

            @pl.when(where_ref[pl.program_id(0)] % parts == p)
            def _(p=p):
                out_ref[0] = taken_ref[:, p * depth : (p + 1) * depth]

    return pl.pallas_call(
        body,
        grid_spec=pltpu.PrefetchScalarGridSpec(
            num_scalar_prefetch=1,
            grid=(many,),
            in_specs=[pl.BlockSpec((tokens, parts * depth), lambda r, where: (0, where[r] // parts))],
            out_specs=pl.BlockSpec((1, tokens, depth), lambda r, where: (r, 0, 0)),
        ),
        out_shape=jax.ShapeDtypeStruct((many, tokens, depth), BF16),
        compiler_params=params(60),
        cost_estimate=cost(0, 4 * tokens * many * depth),
    )(where, activations)


def project(where, taken, slabs, tensor):
    tokens = taken.shape[1] // tensor
    depth, rank = slabs[0].shape
    many = len(slabs)

    def body(where_ref, taken_ref, *refs):
        held, outs = refs[:many], refs[many:]
        total = jnp.dot(taken_ref[0], held[0][...], preferred_element_type=F32)
        for r in range(1, many):
            total += jnp.dot(taken_ref[r], held[r][...], preferred_element_type=F32)
        for j in range(tensor):

            @pl.when(pl.program_id(0) == j)
            def _(j=j):
                outs[j][...] = total.astype(outs[j].dtype)

    whole = pl.BlockSpec((depth, rank), lambda j, where: (0, 0))
    out = pl.BlockSpec((tokens, rank), lambda j, where: (0, 0))
    return pl.pallas_call(
        body,
        grid_spec=pltpu.PrefetchScalarGridSpec(
            num_scalar_prefetch=1,
            grid=(tensor,),
            in_specs=[pl.BlockSpec((many, tokens, depth), lambda j, where: (0, where[j], 0))]
            + [whole] * many,
            out_specs=[out] * tensor,
        ),
        out_shape=[
            jax.ShapeDtypeStruct((tokens, rank), F32 if j == 0 else BF16) for j in range(tensor)
        ],
        compiler_params=params(32),
        cost_estimate=cost(
            2 * tensor * tokens * many * depth * rank, 2 * many * depth * (tensor * tokens + rank)
        ),
    )(where, taken, *slabs)


def flip(where, pieces, chips):
    tokens, rank = pieces[0].shape
    many = len(pieces)
    rows = rank // chips

    def body(where_ref, *refs):
        out = refs[many]
        for j in range(many):
            turned = refs[j][...].T
            at = pl.multiple_of(where_ref[j] * tokens, 128)
            refs[many + 1][...] = turned
            for i in range(chips):
                source = pl.multiple_of(where_ref[many + i] * rows, rows)
                out[pl.ds(i * rows, rows), pl.ds(at, tokens)] = refs[many + 1][pl.ds(source, rows), :]

    return pl.pallas_call(
        body,
        grid_spec=pltpu.PrefetchScalarGridSpec(
            num_scalar_prefetch=1,
            grid=(1,),
            in_specs=[pl.BlockSpec((tokens, rank), lambda i, where: (0, 0))] * many,
            out_specs=pl.BlockSpec((rank, many * tokens), lambda i, where: (0, 0)),
            scratch_shapes=[pltpu.VMEM((rank, tokens), BF16)],
        ),
        out_shape=jax.ShapeDtypeStruct((rank, many * tokens), BF16),
        compiler_params=params(16),
        cost_estimate=cost(0, 4 * rank * tokens * many),
    )(where, *pieces)


def arrange(where, pieces, choose):
    height, rank = pieces[0].shape
    many = len(pieces)

    def body(where_ref, choose_ref, *refs):
        for j in range(many):
            at = pl.multiple_of(where_ref[j] * height, height)
            refs[many][pl.ds(at, height), :] = jnp.dot(
                refs[j][...], choose_ref[...], preferred_element_type=F32
            ).astype(BF16)

    return pl.pallas_call(
        body,
        grid_spec=pltpu.PrefetchScalarGridSpec(
            num_scalar_prefetch=1,
            grid=(1,),
            in_specs=[pl.BlockSpec((rank, rank), lambda i, where: (0, 0))]
            + [pl.BlockSpec((height, rank), lambda i, where: (0, 0))] * many,
            out_specs=pl.BlockSpec((many * height, rank), lambda i, where: (0, 0)),
        ),
        out_shape=jax.ShapeDtypeStruct((many * height, rank), BF16),
        compiler_params=params(16),
        cost_estimate=cost(2 * rank * rank * height * many, 4 * rank * height * many),
    )(where, choose, *pieces)


def unset(shape):
    return pl.pallas_call(
        lambda out_ref: None,
        out_shape=jax.ShapeDtypeStruct(shape, F32),
        out_specs=ANYWHERE,
    )()


def per_device(dp, tensor, activations, out_grad, projector, first_moment, second_moment):
    chips = dp // 2
    dp_at, t_at = lax.axis_index("dp"), lax.axis_index("tensor")
    chip, core = dp_at // 2, dp_at % 2
    behind = jnp.where(core == 0, chip, chips - 1 - chip)
    slots = jnp.arange(chips)
    slot_chip = jnp.where(core == 0, chip + slots, chip - slots + chips) % chips
    peers = t_at ^ jnp.arange(tensor)
    columns = out_grad.shape[1]
    rank = projector.shape[1]
    rows = rank // chips

    def swap(value):
        return lax.ppermute(value, "dp", [(i, i ^ 1) for i in range(dp)])

    def rotate(value, by):
        pairs = [(2 * q + c, 2 * ((q + by) % chips) + c) for q in range(chips) for c in (0, 1)]
        return lax.ppermute(value, "dp", pairs)

    def onward(value):
        up = [(2 * q, 2 * q + 2) for q in range(chips - 1)]
        down = [(2 * q + 3, 2 * q + 1) for q in range(chips - 1)]
        return lax.ppermute(value, "dp", up + down)

    def exchange(value, j):
        return lax.ppermute(value, "tensor", [(t, t ^ j) for t in range(tensor)])

    state = {"last": None}

    def after(*values):
        if state["last"] is None:
            return values
        return lax.optimization_barrier((values, state["last"]))[0]

    def ended(value):
        state["last"] = value
        return value

    slabs = [projector] + [rotate(projector, chips - r) for r in range(1, chips)]
    order = (chip + slots) % chips * 2
    order = jnp.concatenate([order + core, order + 1 - core]) * tensor + t_at
    taken = ended(gather(order.astype(jnp.int32), activations, dp, projector.shape[0]))

    basis = [projector] + [exchange(projector, j) for j in range(1, tensor)]
    wanted = (slot_chip[:, None] * rows + jnp.arange(rows)[None]).reshape(-1)
    choose = (jnp.arange(rank)[:, None] == wanted[None]).astype(BF16)
    (choose,) = after(choose)
    basis = ended(arrange(peers.astype(jnp.int32), basis, choose))

    taken, *slabs[1:] = after(taken, *slabs[1:])
    slabs = slabs + [swap(slab) for slab in slabs]
    parts = project(peers.astype(jnp.int32), taken, slabs, tensor)
    ended(parts[0])
    total = parts[0]
    for j in range(1, tensor):
        total = total + exchange(parts[j], j).astype(F32)
    piece = total.astype(BF16)
    pieces = [piece] + [exchange(piece, j) for j in range(1, tensor)]
    flipped = flip(jnp.concatenate([peers, slot_chip]).astype(jnp.int32), pieces, chips)
    ended(flipped)

    widths = split_widths(columns)
    offsets = [sum(widths[:i]) for i in range(len(widths))]

    def cut(value, k):
        return lax.slice_in_dim(value, offsets[k], offsets[k] + widths[k], axis=1)

    def slot(value, i):
        return lax.slice_in_dim(value, i * rows, (i + 1) * rows, axis=0)

    state["update"] = unset((basis.shape[0], columns))
    state["new_first"], state["new_second"] = unset(first_moment.shape), unset(first_moment.shape)
    pending = []

    def put(name, value, k):
        state[name] = lax.dynamic_update_slice(state[name], value, (0, offsets[k]))

    def encode(k):
        weights, grad = after(flipped, out_grad)
        whole = jnp.dot(weights, cut(grad, k), preferred_element_type=F32).astype(BF16)
        ended(whole)
        return whole, swap(whole)

    def summed(whole, given, got, i, j):
        whole, given, *got = after(whole, given, *([] if got is None else [got]))
        total = slot(whole, i).astype(F32) + slot(given, j).astype(F32)
        for one in got:
            total = total + one.astype(F32)
        return total

    def adam(k, whole, given, got):
        whole, given, got = after(whole, given, got)
        other = swap(got)

        def own_half(value):
            return lax.dynamic_slice_in_dim(value, core * (rows // 2), rows // 2).astype(F32)

        total = own_half(slot(whole, 0)) + own_half(slot(given, 0)) + own_half(got) + own_half(other)
        new_first = beta_one * cut(first_moment, k) + (1.0 - beta_one) * total
        new_second = beta_two * cut(second_moment, k) + (1.0 - beta_two) * total * total
        step = new_first / bias_one / (jnp.sqrt(new_second / bias_two) + adam_eps)
        step = ended(step.astype(BF16))

        def moments():
            values = after(new_first, new_second)
            put("new_first", values[0], k)
            put("new_second", values[1], k)
            ended(state["new_second"])

        pending.append(moments)
        other = swap(step)
        return ended(
            jnp.concatenate([jnp.where(core == 0, step, other), jnp.where(core == 0, other, step)])
        )

    def decode(k, step, arrived, passed):
        step, *values = after(step, *arrived, *passed)
        arrived, passed = values[: chips - 1], values[chips - 1 :]
        pieces = [step] + [
            jnp.where(behind >= chips - i, arrived[chips - 1 - i], passed[i - 1])
            for i in range(1, chips)
        ]
        put("update", jnp.dot(basis, jnp.concatenate(pieces), preferred_element_type=F32), k)
        ended(state["update"])

    def stream(ks):
        before, ahead = None, None
        for k in [*ks, None]:
            if k is not None:
                whole, given = encode(k) if ahead is None else ahead.pop()
                if before is None:
                    yield
                if k != ks[-1]:
                    ahead = []
                    pending.append(lambda ahead=ahead, k=k: ahead.append(encode(ks[ks.index(k) + 1])))
            got = None
            for step in range(chips - 1 if k is not None else chips - 2):
                forward = before is not None and step < chips - 2
                if k is not None:
                    i = chips - 1 - step
                    send = summed(whole, given, got, i, chips - i).astype(BF16)
                    if forward:
                        send = jnp.where(behind <= step, send, before[2][-1])
                    ended(send)
                else:
                    send = before[2][-1]
                got = onward(send)
                if forward:
                    prior, own, arrived, passed = before
                    arrived.append(got)
                    passed.append(swap(*after(got)))
                    if step == chips - 3:
                        pending.append(functools.partial(decode, prior, own, arrived, passed))
                yield
            if k is None:
                return
            own = adam(k, whole, given, got)
            got = onward(own)
            before = (k, own, [got], [swap(got)])
            yield

    running = [stream(list(range(n, len(widths), 2))) for n in range(min(2, len(widths)))]
    started = 0
    while running:
        for one in list(running):
            if next(one, running) is running:
                running.remove(one)
            elif pending and started >= 2:
                pending.pop(0)()
            started += 1
    while pending:
        pending.pop(0)()
    return state["update"], state["new_first"], state["new_second"]


def solution(mesh):
    in_specs = (
        P("dp", None),
        P("dp", "tensor"),
        P(("dp", "tensor"), None),
        P("dp", "tensor"),
        P("dp", "tensor"),
    )
    out_specs = (P("dp", "tensor"), P("dp", "tensor"), P("dp", "tensor"))
    return jax.shard_map(
        functools.partial(per_device, mesh.shape["dp"], mesh.shape["tensor"]),
        mesh=mesh,
        in_specs=in_specs,
        out_specs=out_specs,
        check_vma=False,
    )
```

```python
import functools

import jax
import jax.numpy as jnp
from jax import lax
from jax.experimental import pallas as pl
from jax.experimental.pallas import tpu as pltpu
from jax.sharding import PartitionSpec as P

beta_one = 0.9
beta_two = 0.999
bias_one = 1.0 - 0.9**10
bias_two = 1.0 - 0.999**10
adam_eps = 1e-08

PARTS = 2
HALVES = 2
UNIT = 256
F32 = jnp.float32
BF16 = jnp.bfloat16
ANYWHERE = pl.BlockSpec(memory_space=pl.ANY)


def split_widths(columns):
    units, parts = columns // UNIT, min(PARTS, columns // UNIT)
    more = units % parts if parts == 3 else 0
    return [UNIT * (units // parts + (more if i == 1 else 0) + (parts != 3 and i < units % parts)) for i in range(parts)]


def params(mib):
    return pltpu.CompilerParams(vmem_limit_bytes=mib << 20)


def cost(flops, moved):
    return pl.CostEstimate(flops=flops, bytes_accessed=moved, transcendentals=0)


def gather(where, activations, many, depth):
    tokens = activations.shape[0]
    parts = max(1, 128 // depth)

    def body(where_ref, taken_ref, out_ref):
        for p in range(parts):

            @pl.when(where_ref[pl.program_id(0)] % parts == p)
            def _(p=p):
                out_ref[0] = taken_ref[:, p * depth : (p + 1) * depth]

    return pl.pallas_call(
        body,
        grid_spec=pltpu.PrefetchScalarGridSpec(
            num_scalar_prefetch=1,
            grid=(many,),
            in_specs=[pl.BlockSpec((tokens, parts * depth), lambda r, where: (0, where[r] // parts))],
            out_specs=pl.BlockSpec((1, tokens, depth), lambda r, where: (r, 0, 0)),
        ),
        out_shape=jax.ShapeDtypeStruct((many, tokens, depth), BF16),
        compiler_params=params(60),
        cost_estimate=cost(0, 4 * tokens * many * depth),
    )(where, activations)


def project(where, taken, slabs, tensor):
    tokens = taken.shape[1] // tensor
    depth, rank = slabs[0].shape
    many = len(slabs)

    def body(where_ref, taken_ref, *refs):
        held, outs = refs[:many], refs[many:]
        total = jnp.dot(taken_ref[0], held[0][...], preferred_element_type=F32)
        for r in range(1, many):
            total += jnp.dot(taken_ref[r], held[r][...], preferred_element_type=F32)
        for j in range(tensor):

            @pl.when(pl.program_id(0) == j)
            def _(j=j):
                outs[j][...] = total.astype(outs[j].dtype)

    whole = pl.BlockSpec((depth, rank), lambda j, where: (0, 0))
    out = pl.BlockSpec((tokens, rank), lambda j, where: (0, 0))
    return pl.pallas_call(
        body,
        grid_spec=pltpu.PrefetchScalarGridSpec(
            num_scalar_prefetch=1,
            grid=(tensor,),
            in_specs=[pl.BlockSpec((many, tokens, depth), lambda j, where: (0, where[j], 0))]
            + [whole] * many,
            out_specs=[out] * tensor,
        ),
        out_shape=[
            jax.ShapeDtypeStruct((tokens, rank), F32 if j == 0 else BF16) for j in range(tensor)
        ],
        compiler_params=params(32),
        cost_estimate=cost(
            2 * tensor * tokens * many * depth * rank, 2 * many * depth * (tensor * tokens + rank)
        ),
    )(where, taken, *slabs)


def flip(where, parts, chips):
    many, halves = len(parts[0]), len(parts)
    tokens, width = parts[0][0].shape
    rank = width * halves
    rows = rank // chips

    def body(where_ref, *refs):
        out, stage = refs[-2:]
        for j in range(many):
            at = pl.multiple_of(where_ref[j] * tokens, 128)
            for h in range(halves):
                stage[h * width : (h + 1) * width, :] = refs[h * many + j][...].T
            for i in range(chips):
                source = pl.multiple_of(where_ref[many + i] * rows, rows)
                out[pl.ds(i * rows, rows), pl.ds(at, tokens)] = stage[pl.ds(source, rows), :]

    return pl.pallas_call(
        body,
        grid_spec=pltpu.PrefetchScalarGridSpec(
            num_scalar_prefetch=1,
            grid=(1,),
            in_specs=[pl.BlockSpec((tokens, width), lambda i, where: (0, 0))] * (many * halves),
            out_specs=pl.BlockSpec((rank, many * tokens), lambda i, where: (0, 0)),
            scratch_shapes=[pltpu.VMEM((rank, tokens), BF16)],
        ),
        out_shape=jax.ShapeDtypeStruct((rank, many * tokens), BF16),
        compiler_params=params(16),
        cost_estimate=cost(0, 4 * rank * tokens * many),
    )(where, *[piece for part in parts for piece in part])


def arrange(where, pieces, choose):
    height, rank = pieces[0].shape
    many = len(pieces)

    def body(where_ref, choose_ref, *refs):
        for j in range(many):
            at = pl.multiple_of(where_ref[j] * height, height)
            refs[many][pl.ds(at, height), :] = jnp.dot(
                refs[j][...], choose_ref[...], preferred_element_type=F32
            ).astype(BF16)

    return pl.pallas_call(
        body,
        grid_spec=pltpu.PrefetchScalarGridSpec(
            num_scalar_prefetch=1,
            grid=(1,),
            in_specs=[pl.BlockSpec((rank, rank), lambda i, where: (0, 0))]
            + [pl.BlockSpec((height, rank), lambda i, where: (0, 0))] * many,
            out_specs=pl.BlockSpec((many * height, rank), lambda i, where: (0, 0)),
        ),
        out_shape=jax.ShapeDtypeStruct((many * height, rank), BF16),
        compiler_params=params(16),
        cost_estimate=cost(2 * rank * rank * height * many, 4 * rank * height * many),
    )(where, choose, *pieces)


def unset(shape):
    return pl.pallas_call(
        lambda out_ref: None,
        out_shape=jax.ShapeDtypeStruct(shape, F32),
        out_specs=ANYWHERE,
    )()


def per_device(dp, tensor, activations, out_grad, projector, first_moment, second_moment):
    chips = dp // 2
    dp_at, t_at = lax.axis_index("dp"), lax.axis_index("tensor")
    chip, core = dp_at // 2, dp_at % 2
    behind = jnp.where(core == 0, chip, chips - 1 - chip)
    slots = jnp.arange(chips)
    slot_chip = jnp.where(core == 0, chip + slots, chip - slots + chips) % chips
    peers = t_at ^ jnp.arange(tensor)
    columns = out_grad.shape[1]
    rank = projector.shape[1]
    rows = rank // chips

    def swap(value):
        return lax.ppermute(value, "dp", [(i, i ^ 1) for i in range(dp)])

    def rotate(value, by):
        pairs = [(2 * q + c, 2 * ((q + by) % chips) + c) for q in range(chips) for c in (0, 1)]
        return lax.ppermute(value, "dp", pairs)

    def onward(value):
        up = [(2 * q, 2 * q + 2) for q in range(chips - 1)]
        down = [(2 * q + 3, 2 * q + 1) for q in range(chips - 1)]
        return lax.ppermute(value, "dp", up + down)

    def exchange(value, j):
        return lax.ppermute(value, "tensor", [(t, t ^ j) for t in range(tensor)])

    state = {"last": None}

    def after(*values):
        if state["last"] is None:
            return values
        return lax.optimization_barrier((values, state["last"]))[0]

    def ended(value):
        state["last"] = value
        return value

    width = rank // HALVES
    slabs = []
    for h in range(HALVES):
        own = projector[:, h * width : (h + 1) * width]
        slabs.append([own] + [rotate(own, chips - r) for r in range(1, chips)])
    order = (chip + slots) % chips * 2
    order = jnp.concatenate([order + core, order + 1 - core]) * tensor + t_at
    taken = ended(gather(order.astype(jnp.int32), activations, dp, projector.shape[0]))

    basis = [projector] + [exchange(projector, j) for j in range(1, tensor)]
    wanted = (slot_chip[:, None] * rows + jnp.arange(rows)[None]).reshape(-1)
    choose = (jnp.arange(rank)[:, None] == wanted[None]).astype(BF16)
    (choose,) = after(choose)
    basis = ended(arrange(peers.astype(jnp.int32), basis, choose))

    gathered = []
    for held in slabs:
        taken, *held[1:] = after(taken, *held[1:])
        held = held + [swap(slab) for slab in held]
        parts = project(peers.astype(jnp.int32), taken, held, tensor)
        ended(parts[0])
        total = parts[0]
        for j in range(1, tensor):
            total = total + exchange(parts[j], j).astype(F32)
        piece = total.astype(BF16)
        gathered.append([piece] + [exchange(piece, j) for j in range(1, tensor)])
    flipped = flip(jnp.concatenate([peers, slot_chip]).astype(jnp.int32), gathered, chips)
    ended(flipped)

    widths = split_widths(columns)
    offsets = [sum(widths[:i]) for i in range(len(widths))]

    def cut(value, k):
        return lax.slice_in_dim(value, offsets[k], offsets[k] + widths[k], axis=1)

    def slot(value, i):
        return lax.slice_in_dim(value, i * rows, (i + 1) * rows, axis=0)

    state["update"] = unset((basis.shape[0], columns))
    state["new_first"], state["new_second"] = unset(first_moment.shape), unset(first_moment.shape)
    pending = []

    def put(name, value, k):
        state[name] = lax.dynamic_update_slice(state[name], value, (0, offsets[k]))

    def encode(k):
        weights, grad = after(flipped, out_grad)
        whole = jnp.dot(weights, cut(grad, k), preferred_element_type=F32).astype(BF16)
        ended(whole)
        return whole, swap(whole)

    def summed(whole, given, got, i, j):
        whole, given, *got = after(whole, given, *([] if got is None else [got]))
        total = slot(whole, i).astype(F32) + slot(given, j).astype(F32)
        for one in got:
            total = total + one.astype(F32)
        return total

    def adam(k, whole, given, got):
        whole, given, got = after(whole, given, got)
        other = swap(got)

        def own_half(value):
            return lax.dynamic_slice_in_dim(value, core * (rows // 2), rows // 2).astype(F32)

        total = own_half(slot(whole, 0)) + own_half(slot(given, 0)) + own_half(got) + own_half(other)
        new_first = beta_one * cut(first_moment, k) + (1.0 - beta_one) * total
        new_second = beta_two * cut(second_moment, k) + (1.0 - beta_two) * total * total
        step = new_first / bias_one / (jnp.sqrt(new_second / bias_two) + adam_eps)
        step = ended(step.astype(BF16))

        def moments():
            values = after(new_first, new_second)
            put("new_first", values[0], k)
            put("new_second", values[1], k)
            ended(state["new_second"])

        pending.append(moments)
        other = swap(step)
        return ended(
            jnp.concatenate([jnp.where(core == 0, step, other), jnp.where(core == 0, other, step)])
        )

    def decode(k, step, arrived, passed):
        step, *values = after(step, *arrived, *passed)
        arrived, passed = values[: chips - 1], values[chips - 1 :]
        pieces = [step] + [
            jnp.where(behind >= chips - i, arrived[chips - 1 - i], passed[i - 1])
            for i in range(1, chips)
        ]
        put("update", jnp.dot(basis, jnp.concatenate(pieces), preferred_element_type=F32), k)
        ended(state["update"])

    def stream(ks):
        before, ahead = None, None
        for k in [*ks, None]:
            if k is not None:
                whole, given = encode(k) if ahead is None else ahead.pop()
                if before is None:
                    yield
                if k != ks[-1]:
                    ahead = []
                    pending.append(lambda ahead=ahead, k=k: ahead.append(encode(ks[ks.index(k) + 1])))
            got = None
            for step in range(chips - 1 if k is not None else chips - 2):
                forward = before is not None and step < chips - 2
                if k is not None:
                    i = chips - 1 - step
                    send = summed(whole, given, got, i, chips - i).astype(BF16)
                    if forward:
                        send = jnp.where(behind <= step, send, before[2][-1])
                    ended(send)
                else:
                    send = before[2][-1]
                got = onward(send)
                if forward:
                    prior, own, arrived, passed = before
                    arrived.append(got)
                    passed.append(swap(*after(got)))
                    if step == chips - 3:
                        pending.append(functools.partial(decode, prior, own, arrived, passed))
                yield
            if k is None:
                return
            own = adam(k, whole, given, got)
            got = onward(own)
            before = (k, own, [got], [swap(got)])
            yield

    running = [stream(list(range(n, len(widths), 2))) for n in range(min(2, len(widths)))]
    started = 0
    while running:
        for one in list(running):
            if next(one, running) is running:
                running.remove(one)
            elif pending and started >= 2:
                pending.pop(0)()
            started += 1
    while pending:
        pending.pop(0)()
    return state["update"], state["new_first"], state["new_second"]


def solution(mesh):
    in_specs = (
        P("dp", None),
        P("dp", "tensor"),
        P(("dp", "tensor"), None),
        P("dp", "tensor"),
        P("dp", "tensor"),
    )
    out_specs = (P("dp", "tensor"), P("dp", "tensor"), P("dp", "tensor"))
    return jax.shard_map(
        functools.partial(per_device, mesh.shape["dp"], mesh.shape["tensor"]),
        mesh=mesh,
        in_specs=in_specs,
        out_specs=out_specs,
        check_vma=False,
    )
```
